32 devices in a mesh: dp: 4 (over x, core), expert: 8 (over z, y).
Axes of the slice: x: 2, y: 2, z: 4, core: 2. Of those that a mesh axis runs over, the one named last changes fastest.
Arguments:
- tokens: bfloat16 [4096, 2048], P(('dp', 'expert')), may hold values from -6 to 6
- out_grad: bfloat16 [4096, 2048], P(('dp', 'expert')), may hold values from -6 to 6
- w_in: bfloat16 [2048, 512], replicated, may hold values from -0.125 to 0.125
- w_out: bfloat16 [512, 2048], replicated, may hold values from -0.25 to 0.25
- w_gate: bfloat16 [8, 512, 1024], P('expert'), may hold values from -0.25 to 0.25
- w_up: bfloat16 [8, 512, 1024], P('expert'), may hold values from -0.25 to 0.25
- w_down: bfloat16 [8, 1024, 512], P('expert'), may hold values from -0.1875 to 0.1875
- gate_logits: float32 [4096, 2], P(('dp', 'expert')), may hold values from -8 to 8
- expert_ids: int32 [4096, 2], P(('dp', 'expert')), may hold values from 0 to 7, all different within a row; in each aligned block of 128 rows (0 to 127, 128 to 255, ...) at most 48 rows name the same one
Outputs:
- token_grad: bfloat16 [4096, 2048], P(('dp', 'expert'))
- logit_grad: float32 [4096, 2], P(('dp', 'expert'))
- grad_in: float32 [8, 2048, 512], P('expert', 'dp')
- grad_out: float32 [8, 512, 2048], P('expert', None, 'dp')
The draws below stay inside these ranges and needn't reach their ends.
Inputs may be any that keep to these rules, and one draw needn't show every extreme that they name: `expert_ids`: each row names 2 different experts. Among the 128 rows of one device (aligned blocks) no expert is named more than 48 times, a bound that some block reaches.
All inputs are finite; a program needn't handle non-finite values.
Results may differ from the reference program's by a relative error of at most 0.01.
Values may be sent and summed in bfloat16 or wider, within the bound.
A program may use at most 64 MiB of HBM per device.

```python
import math
import jax
import jax.numpy as jnp
import numpy as np
from jax import lax

D = 2048
L = 512
H = 1024
TOP = 2
TOK_DEV = 128
EXPERTS = 8
CAP = 48
TOKENS = 4096
N_DP = 4
N_EXPERT = 8
DEVICES = 32


def strengthened(entries, rng, source, target, parts, factor):
    owner, partner = [(jnp.arange(entries.shape[axis_at]) // (entries.shape[axis_at] // parts)).reshape([-1 if axis == axis_at else 1 for axis in range(entries.ndim)]) for axis_at in (source, target)]
    chosen = jax.random.permutation(rng, parts)[partner]
    strong = (owner == chosen) | (owner == (partner + parts // 2) % parts)
    return jnp.where(strong, factor * entries, entries)


def steps_of(key, shape, cuts, smallest, top_value):
    loudness, own = 1.0, jax.random.fold_in(key, 6)
    for axis_at, parts in cuts:
        draws = jnp.exp(jax.random.uniform(jax.random.fold_in(own, axis_at), (parts,), jnp.float32, smallest / len(cuts), top_value / len(cuts)))
        loudness = loudness * jnp.repeat(draws, shape[axis_at] // parts).reshape([-1 if axis == axis_at else 1 for axis in range(len(shape))])
    return loudness


def routed_block(stream_key, own, number, rows, amount, top, bound, skew):
    order = jax.random.permutation(stream_key, amount)
    heavy_load, common = portions_of(amount, rows * top, bound, skew, True), portions_of(amount, rows * top, bound, skew, False)
    places = jnp.arange(amount)

    def named(tallies, rotation):
        used = int((tallies > 0).sum())
        fixed = max(1, used // 4)
        shifted = fixed + (places - fixed + rotation * (used - fixed)) % max(1, amount - fixed)
        return jnp.zeros((amount,), jnp.int32).at[order[jnp.where(places < fixed, places, shifted)]].set(jnp.asarray(tallies, jnp.int32))

    tallies = jnp.where(number % 4 == 0, named(heavy_load, number // 4), named(common, number - number // 4 - 1))
    mixed = jax.random.permutation(jax.random.fold_in(own, 3), amount)
    giver, taker = mixed[0:amount // 2 * 2:2], mixed[1:amount // 2 * 2:2]
    margin = jnp.minimum(tallies[giver] - 1, bound - tallies[taker]) // 2
    margin = jnp.where((giver == order[0]) | (taker == order[0]) | (tallies[taker] == 0), 0, jnp.maximum(margin, 0))
    shifted = jax.random.randint(jax.random.fold_in(own, 4), (amount // 2,), 0, 1 << 20) % (margin + 1)
    tallies = tallies.at[giver].add(-shifted).at[taker].add(shifted)
    members = jnp.searchsorted(jnp.cumsum(tallies), jnp.arange(rows * top), side="right").astype(jnp.int32)
    table = members.reshape(top, rows).T
    table = table[jax.random.permutation(jax.random.fold_in(own, 1), rows)]
    rotation = jax.random.randint(jax.random.fold_in(own, 2), (rows, 1), 0, top)
    return jnp.take_along_axis(table, (jnp.arange(top)[None, :] + rotation) % top, axis=1)


def portions_of(count, total, reach, lean, full):
    loads = [(1 << 20) // math.isqrt(rank ** lean) + 1 for rank in range(1, count + 1)]
    largest = reach if full else min(reach, max(-(-total // count), total * loads[0] // sum(loads)))
    least = 1 if total - largest >= count - 1 else 0
    given, spare = [largest] + [least] * (count - 1), total - largest - least * (count - 1)
    while spare > 0:
        movable = [i for i in range(1, count) if given[i] < largest] or [i for i in range(1, count) if given[i] < reach]
        pool, budget = sum([loads[i] for i in movable]), spare
        for i in movable:
            extra = min(reach - given[i], max(1, budget * loads[i] // pool), spare)
            given[i] = given[i] + extra
            spare = spare - extra
    return np.array(given)


def scatter_about(stream_key, dims, scale, reach, cuts=(), kind=jnp.bfloat16):
    level = steps_of(stream_key, dims, cuts, -0.22, 0.18) if cuts else 1.0
    result = jax.random.normal(stream_key, dims, jnp.float32) * scale * level
    return jnp.minimum(jnp.maximum(result, -reach), reach).astype(kind)


def bell_draw_with(own_key, extent, scale, bound, cuts, heavy, kind=jnp.bfloat16):
    array = scale * jax.random.normal(own_key, extent, jnp.float32)
    if cuts:
        array = array * steps_of(own_key, extent, cuts, -0.22, 0.18)
    return jnp.clip(strengthened(array, jax.random.fold_in(own_key, 3), *heavy), -bound, bound).astype(kind)


def setup_inputs(seed: int = 0) -> dict:
    key_of = jax.random.split(jax.random.key(seed), 10)
    tokens = bell_draw_with(key_of[0], (TOKENS, D), 1.0, 6.0, ((0, 32),), (0, 1, 32, 2.75))
    out_grad = bell_draw_with(key_of[1], (TOKENS, D), 1.0, 6.0, ((0, 32),), (0, 1, 32, 2.75))
    w_in = scatter_about(key_of[2], (D, L), D ** -0.5, 0.125)
    w_out = scatter_about(key_of[3], (L, D), L ** -0.5, 0.25)
    w_gate = scatter_about(key_of[4], (EXPERTS, L, H), L ** -0.5, 0.25, ((0, 8),))
    w_up = scatter_about(key_of[5], (EXPERTS, L, H), L ** -0.5, 0.25, ((0, 8),))
    w_down = scatter_about(key_of[6], (EXPERTS, H, L), H ** -0.5, 0.1875, ((0, 8),))
    gate_logits = scatter_about(key_of[7], (TOKENS, TOP), 2.0, 8.0, ((0, 32),), jnp.float32)
    expert_ids_keys = jax.random.split(jax.random.fold_in(key_of[8], 1), TOKENS // TOK_DEV)
    expert_ids_turns = jax.random.permutation(jax.random.fold_in(key_of[8], 3), TOKENS // TOK_DEV)
    expert_ids = jax.vmap(lambda own, number: routed_block(jax.random.fold_in(key_of[8], 2), own, number, TOK_DEV, EXPERTS, TOP, CAP, 2))(expert_ids_keys, expert_ids_turns).reshape((TOKENS, TOP))
    return {"tokens": tokens, "out_grad": out_grad, "w_in": w_in, "w_out": w_out, "w_gate": w_gate, "w_up": w_up, "w_down": w_down, "gate_logits": gate_logits, "expert_ids": expert_ids}


def expert_pass(pieces):
    z_rows, g_rows, wg, wu, wd = pieces
    pre_a = jnp.dot(z_rows, wg, preferred_element_type=jnp.float32)
    pre_b = jnp.dot(z_rows, wu, preferred_element_type=jnp.float32)
    sig = jax.nn.sigmoid(pre_a)
    hidden = (pre_a * sig * pre_b).astype(jnp.bfloat16)
    outv = jnp.dot(hidden, wd, preferred_element_type=jnp.float32).astype(jnp.bfloat16)
    hid_grad = jnp.dot(g_rows, wd.T, preferred_element_type=jnp.float32)
    grad_a = (hid_grad * pre_b * sig * (1.0 + pre_a * (1.0 - sig))).astype(jnp.bfloat16)
    grad_b = (hid_grad * pre_a * sig).astype(jnp.bfloat16)
    grad_z = jnp.dot(grad_a, wg.T, preferred_element_type=jnp.float32) + jnp.dot(grad_b, wu.T, preferred_element_type=jnp.float32)
    return outv, grad_z.astype(jnp.bfloat16)


def reference(tokens, out_grad, w_in, w_out, w_gate, w_up, w_down, gate_logits, expert_ids):
    latent = jnp.dot(tokens, w_in, preferred_element_type=jnp.float32).astype(jnp.bfloat16)
    lat_grad = jnp.dot(out_grad, w_out.T, preferred_element_type=jnp.float32).astype(jnp.bfloat16)
    score = jax.nn.sigmoid(gate_logits.astype(jnp.float32))
    total = jnp.sum(score, axis=1, keepdims=True)
    gate = score / total
    ids = expert_ids.reshape(DEVICES, TOK_DEV * TOP)
    onehot = (ids[:, :, None] == jnp.arange(EXPERTS, dtype=jnp.int32)[None, None, :]).astype(jnp.int32)
    rank = jnp.cumsum(onehot, axis=1) - onehot
    slot = jnp.sum(rank * onehot, axis=2)
    row = jnp.arange(DEVICES, dtype=jnp.int32)[:, None] * CAP + slot
    flat_ids = ids.reshape(-1)
    flat_rows = row.reshape(-1).astype(jnp.int32)
    source = jnp.arange(TOKENS * TOP, dtype=jnp.int32) // TOP
    z_buf = jnp.zeros((EXPERTS, DEVICES * CAP, L), jnp.bfloat16).at[flat_ids, flat_rows].set(latent[source])
    g_buf = jnp.zeros((EXPERTS, DEVICES * CAP, L), jnp.bfloat16).at[flat_ids, flat_rows].set(lat_grad[source])
    out_buf, grad_buf = lax.map(expert_pass, (z_buf, g_buf, w_gate, w_up, w_down))
    expert_out = out_buf[flat_ids, flat_rows].reshape(TOKENS, TOP, L).astype(jnp.float32)
    choice_grad = grad_buf[flat_ids, flat_rows].reshape(TOKENS, TOP, L).astype(jnp.float32)
    mixed = jnp.sum(gate[:, :, None] * expert_out, axis=1).astype(jnp.bfloat16)
    gate_grad = jnp.sum(expert_out * lat_grad.astype(jnp.float32)[:, None, :], axis=2)
    centred = gate_grad - jnp.sum(gate * gate_grad, axis=1, keepdims=True)
    logit_grad = score * (1.0 - score) * centred / total
    latent_grad = jnp.sum(gate[:, :, None] * choice_grad, axis=1).astype(jnp.bfloat16)
    token_grad = jnp.dot(latent_grad, w_in.T, preferred_element_type=jnp.float32).astype(jnp.bfloat16)
    tok_blocks = tokens.reshape(N_DP, N_EXPERT, TOK_DEV, D)
    dy_blocks = out_grad.reshape(N_DP, N_EXPERT, TOK_DEV, D)
    lg_blocks = latent_grad.reshape(N_DP, N_EXPERT, TOK_DEV, L)
    mix_blocks = mixed.reshape(N_DP, N_EXPERT, TOK_DEV, L)

    def group_sums(pieces):
        xs, dys, lgs, mxs = pieces
        part_in = jnp.einsum("itd,itl->idl", xs.astype(jnp.float32), lgs.astype(jnp.float32))
        part_out = jnp.einsum("itl,itd->ild", mxs.astype(jnp.float32), dys.astype(jnp.float32))
        sum_in = jnp.sum(part_in.astype(jnp.bfloat16).astype(jnp.float32), axis=0)
        sum_out = jnp.sum(part_out.astype(jnp.bfloat16).astype(jnp.float32), axis=0)
        return sum_in, sum_out

    grad_in, grad_out = lax.map(group_sums, (jnp.swapaxes(tok_blocks, 0, 1), jnp.swapaxes(dy_blocks, 0, 1), jnp.swapaxes(lg_blocks, 0, 1), jnp.swapaxes(mix_blocks, 0, 1)))
    return token_grad, logit_grad, grad_in, grad_out
```

```python
import functools

import jax
import jax.numpy as jnp
from jax import lax
from jax.experimental import pallas as pl
from jax.experimental.pallas import tpu as pltpu
from jax.sharding import PartitionSpec as P

BF16 = jnp.bfloat16
F32 = jnp.float32
MESH = pl.DeviceIdType.MESH


def dot(a, b, ca=1, cb=0):
    return lax.dot_general(a, b, (((ca,), (cb,)), ((), ())), preferred_element_type=F32)


def flip(me, k, n):
    out, bit = 0, 1
    while bit < n:
        mine = lax.rem(me // bit, 2)
        out = out + (1 - mine if (k // bit) % 2 else mine) * bit
        bit *= 2
    return out


def kernel(
    n_e, n_dp, cap,
    tokens_h, dy_h, w_in_h, w_out_h, wg_h, wu_h, wd_h, logits, ids,
    tg_h, logit_grad, gin_h, gout_h,
    tokens, dy, w_in, w_out, wg, wu, wd,
    q, lat_grad,
    z_send, g_send, o_send, c_send, z_recv, g_recv, o_recv, c_recv,
    pre_a, pre_b, hid, ga, gb,
    tok_all, dy_all, mix_all, lg_all,
    tg, gin, gout,
    load_sem, own_sem, ssem, rsem, tssem, trsem, mssem, mrsem, lssem, lrsem, out_sem,
):
    rows, top = ids.shape
    slots = n_e * cap
    lat = w_in.shape[1]
    hidden = wg.shape[1]
    dw = tok_all.shape[1]
    me = lax.axis_index("expert")
    dp = lax.axis_index("dp")
    n_x = n_dp // 2
    x, c = dp // 2, lax.rem(dp, 2)

    loads = []
    for i, (src, dst) in enumerate((
        (tokens_h, tokens), (w_in_h, w_in), (dy_h, dy), (w_out_h, w_out),
        (wg_h.at[0], wg), (wu_h.at[0], wu), (wd_h.at[0], wd),
    )):
        load = pltpu.make_async_copy(src, dst, load_sem.at[i])
        load.start()
        loads.append(load)

    barrier = pltpu.get_barrier_semaphore()
    for k in range(1, n_e):
        pl.semaphore_signal(barrier, inc=1, device_id={"expert": flip(me, k, n_e)}, device_id_type=MESH)
    for k in range(1, n_dp):
        pl.semaphore_signal(barrier, inc=1, device_id={"dp": lax.rem(dp + k, n_dp)}, device_id_type=MESH)

    wide = -(-n_e // 128) * 128
    idv = ids[...]
    lane = lax.broadcasted_iota(jnp.int32, (rows, wide), 1)
    hots = [(idv[:, k:k + 1] == lane).astype(F32) for k in range(top)]
    below = lax.broadcasted_iota(jnp.int32, (rows, rows), 1) < lax.broadcasted_iota(jnp.int32, (rows, rows), 0)
    rank = dot(below.astype(BF16), sum(hots[1:], hots[0]).astype(BF16))
    slot_lane = lax.broadcasted_iota(jnp.int32, (rows, slots), 1)
    both = jnp.zeros((rows, slots), F32)
    for k in range(top):
        slot = jnp.sum(hots[k] * rank, axis=1, keepdims=True).astype(jnp.int32)
        hit = (slot_lane == idv[:, k:k + 1] * cap + slot).astype(F32)
        q[k] = hit.astype(BF16)
        both = both + hit
    spread = both.T.astype(BF16)
    score = jax.nn.sigmoid(logits[...])
    total = jnp.sum(score, axis=1, keepdims=True)
    gate = score / total

    pieces = [pl.ds(pl.multiple_of(flip(me, k, n_e) * cap, cap), cap) for k in range(n_e)]
    order = list(range(n_e - 1, 0, -1))

    def exchange(phase, src, dst):
        own = pltpu.make_async_copy(src.at[pieces[0]], dst.at[pieces[0]], own_sem.at[phase])
        copies = [
            pltpu.make_async_remote_copy(
                src_ref=src.at[pieces[k]], dst_ref=dst.at[pieces[0]],
                send_sem=ssem.at[phase, k], recv_sem=rsem.at[phase, k],
                device_id={"expert": flip(me, k, n_e)}, device_id_type=MESH,
            )
            for k in order
        ]
        for copy in copies:
            copy.start()
        own.start()
        return own, copies

    def arrived(pair):
        pair[0].wait()
        for copy in pair[1]:
            copy.wait_recv()

    def block(i):
        return pl.ds(pl.multiple_of(i * rows, rows), rows)

    loads[0].wait()
    loads[1].wait()
    latent = dot(tokens[...], w_in[...]).astype(BF16)
    z_send[...] = dot(spread, latent).astype(BF16)
    pl.semaphore_wait(barrier, n_e + n_dp - 2)
    z_pair = exchange(0, z_send, z_recv)
    loads[2].wait()
    loads[3].wait()
    lat_grad[...] = dot(dy[...], w_out[...], 1, 1).astype(BF16)
    g_send[...] = dot(spread, lat_grad[...]).astype(BF16)
    g_pair = exchange(1, g_send, g_recv)

    slices = []
    for k in range(1, n_dp):
        peer = lax.rem(dp + k, n_dp)
        cols = pl.ds(pl.multiple_of(peer * dw, dw), dw)
        for j, (src, dst) in enumerate(((tokens, tok_all), (dy, dy_all))):
            copy = pltpu.make_async_remote_copy(
                src_ref=src.at[:, cols], dst_ref=dst.at[block(dp)],
                send_sem=tssem.at[j, k], recv_sem=trsem.at[j, k],
                device_id={"dp": peer}, device_id_type=MESH,
            )
            copy.start()
            slices.append(copy)
    mine = pl.ds(pl.multiple_of(dp * dw, dw), dw)
    tok_all[block(dp), :] = tokens[:, mine]
    dy_all[block(dp), :] = dy[:, mine]

    tile = min(256, hidden)
    loads[4].wait()
    loads[5].wait()
    loads[6].wait()
    arrived(z_pair)
    for t in range(hidden // tile):
        cut = slice(t * tile, (t + 1) * tile)
        a = dot(z_recv[...], wg[:, cut])
        b = dot(z_recv[...], wu[:, cut])
        pre_a[:, cut] = a
        pre_b[:, cut] = b
        hid[:, cut] = (a * jax.nn.sigmoid(a) * b).astype(BF16)
    o_send[...] = dot(hid[...], wd[...]).astype(BF16)
    o_pair = exchange(2, o_send, o_recv)

    arrived(g_pair)
    for t in range(hidden // tile):
        cut = slice(t * tile, (t + 1) * tile)
        h = dot(g_recv[...], wd[cut, :], 1, 1)
        a, b = pre_a[:, cut], pre_b[:, cut]
        sg = jax.nn.sigmoid(a)
        ga[:, cut] = (h * b * sg * (1.0 + a * (1.0 - sg))).astype(BF16)
        gb[:, cut] = (h * a * sg).astype(BF16)
    c_send[...] = (dot(ga[...], wg[...], 1, 1) + dot(gb[...], wu[...], 1, 1)).astype(BF16)
    c_pair = exchange(3, c_send, c_recv)

    def share(buf, ss, rs):
        def send(origin, target, k):
            copy = pltpu.make_async_remote_copy(
                src_ref=buf.at[block(origin)], dst_ref=buf.at[block(origin)],
                send_sem=ss.at[k], recv_sem=rs.at[k],
                device_id={"dp": target}, device_id_type=MESH,
            )
            copy.start()
            return copy

        across = [send(dp, lax.rem(x + d, n_x) * 2 + c, d) for d in range(1, n_x)]
        pair = [send(dp, x * 2 + 1 - c, n_x)]
        return across, pair, send

    def pass_on(shared):
        across, pair, send = shared
        for d in range(1, n_x):
            across[d - 1].wait_recv()
            pair.append(send(lax.rem(x - d + n_x, n_x) * 2 + c, x * 2 + 1 - c, n_x + d))
        return across + pair

    arrived(o_pair)
    mixed = jnp.zeros((rows, lat), F32)
    lgf = lat_grad[...].astype(F32)
    gate_grads = []
    for k in range(top):
        back = dot(q[k], o_recv[...])
        mixed = mixed + gate[:, k:k + 1] * back
        gate_grads.append(jnp.sum(back * lgf, axis=1, keepdims=True))
    mix_all[block(dp), :] = mixed.astype(BF16)
    mix_share = share(mix_all, mssem, mrsem)
    mean = sum(gate[:, k:k + 1] * gate_grads[k] for k in range(top))
    column = lax.broadcasted_iota(jnp.int32, (rows, top), 1)
    gate_grad = jnp.zeros((rows, top), F32)
    for k in range(top):
        gate_grad = jnp.where(column == k, gate_grads[k], gate_grad)
    logit_grad[...] = score * (1.0 - score) * (gate_grad - mean) / total
    mix_sent = pass_on(mix_share)
    for copy in slices:
        copy.wait_recv()
    for copy in mix_sent[n_x - 1:]:
        copy.wait_recv()
    gout[...] = dot(mix_all[...], dy_all[...], 0, 0)
    out2 = pltpu.make_async_copy(gout, gout_h.at[0], out_sem.at[2])
    out2.start()

    arrived(c_pair)
    total_grad = jnp.zeros((rows, lat), F32)
    for k in range(top):
        total_grad = total_grad + gate[:, k:k + 1] * dot(q[k], c_recv[...])
    latent_grad = total_grad.astype(BF16)
    lg_all[block(dp), :] = latent_grad
    lg_share = share(lg_all, lssem, lrsem)
    tg[...] = dot(latent_grad, w_in[...], 1, 1).astype(BF16)
    out0 = pltpu.make_async_copy(tg, tg_h, out_sem.at[0])
    out0.start()
    lg_sent = pass_on(lg_share)
    for copy in lg_sent[n_x - 1:]:
        copy.wait_recv()
    gin[...] = dot(tok_all[...], lg_all[...], 0, 0)
    out1 = pltpu.make_async_copy(gin, gin_h.at[0], out_sem.at[1])
    out1.start()

    for pair in (z_pair, g_pair, o_pair, c_pair):
        for copy in pair[1]:
            copy.wait_send()
    for copy in slices + mix_sent + lg_sent:
        copy.wait_send()
    out2.wait()
    out0.wait()
    out1.wait()


def body(n_e, n_dp, tokens, out_grad, w_in, w_out, w_gate, w_up, w_down, gate_logits, expert_ids):
    rows, width = tokens.shape
    top = expert_ids.shape[1]
    lat = w_in.shape[1]
    hidden = w_gate.shape[2]
    assert w_gate.shape[0] == 1 and n_dp % 2 == 0
    cap = 3 * rows * top // (2 * n_e)
    cap = -(-cap // 16) * 16
    slots = n_e * cap
    dw = width // n_dp
    any_ = pl.BlockSpec(memory_space=pl.ANY)
    vmem = pl.BlockSpec(memory_space=pltpu.VMEM)
    V = pltpu.VMEM
    dma = pltpu.SemaphoreType.DMA
    return pl.pallas_call(
        functools.partial(kernel, n_e, n_dp, cap),
        out_shape=(
            jax.ShapeDtypeStruct((rows, width), BF16),
            jax.ShapeDtypeStruct((rows, top), F32),
            jax.ShapeDtypeStruct((1, dw, lat), F32),
            jax.ShapeDtypeStruct((1, lat, dw), F32),
        ),
        in_specs=[any_] * 7 + [vmem] * 2,
        out_specs=(any_, vmem, any_, any_),
        scratch_shapes=[
            V((rows, width), BF16), V((rows, width), BF16),
            V((width, lat), BF16), V((lat, width), BF16),
            V((lat, hidden), BF16), V((lat, hidden), BF16), V((hidden, lat), BF16),
            V((top, rows, slots), BF16), V((rows, lat), BF16),
            *[V((slots, lat), BF16)] * 8,
            V((slots, hidden), F32), V((slots, hidden), F32),
            V((slots, hidden), BF16), V((slots, hidden), BF16), V((slots, hidden), BF16),
            V((n_dp * rows, dw), BF16), V((n_dp * rows, dw), BF16),
            V((n_dp * rows, lat), BF16), V((n_dp * rows, lat), BF16),
            V((rows, width), BF16), V((dw, lat), F32), V((lat, dw), F32),
            dma((7,)), dma((4,)), dma((4, n_e)), dma((4, n_e)),
            dma((2, n_dp)), dma((2, n_dp)),
            dma((n_dp,)), dma((n_dp,)), dma((n_dp,)), dma((n_dp,)), dma((3,)),
        ],
        compiler_params=pltpu.CompilerParams(
            collective_id=0, has_side_effects=True, vmem_limit_bytes=56 * 1024 * 1024
        ),
    )(tokens, out_grad, w_in, w_out, w_gate, w_up, w_down, gate_logits, expert_ids)


def solution(mesh):
    placed = (
        P(("dp", "expert"), None),
        P(("dp", "expert"), None),
        P(),
        P(),
        P("expert", None, None),
        P("expert", None, None),
        P("expert", None, None),
        P(("dp", "expert"), None),
        P(("dp", "expert"), None),
    )
    return jax.shard_map(
        functools.partial(body, mesh.shape["expert"], mesh.shape["dp"]),
        mesh=mesh,
        in_specs=placed,
        out_specs=(
            P(("dp", "expert"), None),
            P(("dp", "expert"), None),
            P("expert", "dp", None),
            P("expert", None, "dp"),
        ),
        check_vma=False,
    )
```

```python
import functools

import jax
import jax.numpy as jnp
from jax import lax
from jax.experimental import pallas as pl
from jax.experimental.pallas import tpu as pltpu
from jax.sharding import PartitionSpec as P

BF16 = jnp.bfloat16
F32 = jnp.float32
MESH = pl.DeviceIdType.MESH


def dot(a, b, ca=1, cb=0):
    return lax.dot_general(a, b, (((ca,), (cb,)), ((), ())), preferred_element_type=F32)


def flip(me, k, n):
    out, bit = 0, 1
    while bit < n:
        mine = lax.rem(me // bit, 2)
        out = out + (1 - mine if (k // bit) % 2 else mine) * bit
        bit *= 2
    return out


def kernel(
    n_e, n_dp, cap,
    tokens_h, dy_h, w_in_h, w_out_h, wg_h, wu_h, wd_h, logits, ids,
    logit_grad, tok_all, dy_all, mix_all, lg_all,
    tokens, dy, w_in, w_out, wg, wu, wd,
    q, lat_grad,
    z_send, g_send, o_send, c_send, z_recv, g_recv, o_recv, c_recv,
    pre_a, pre_b, hid, ga, gb,
    mix, lg,
    load_sem, own_sem, ssem, rsem, tssem, trsem, mssem, mrsem, lssem, lrsem, out_sem,
):
    top, rows = ids.shape
    slots = n_e * cap
    lat = w_in.shape[1]
    hidden = wg.shape[1]
    dw = tok_all.shape[1]
    me = lax.axis_index("expert")
    dp = lax.axis_index("dp")
    n_x = n_dp // 2
    x, c = dp // 2, lax.rem(dp, 2)

    loads = []
    for i, (src, dst) in enumerate((
        (tokens_h, tokens), (w_in_h, w_in), (dy_h, dy), (w_out_h, w_out),
        (wg_h.at[0], wg), (wu_h.at[0], wu), (wd_h.at[0], wd),
    )):
        load = pltpu.make_async_copy(src, dst, load_sem.at[i])
        load.start()
        loads.append(load)

    barrier = pltpu.get_barrier_semaphore()
    for k in range(1, n_e):
        pl.semaphore_signal(barrier, inc=1, device_id={"expert": flip(me, k, n_e)}, device_id_type=MESH)
    for k in range(1, n_dp):
        pl.semaphore_signal(barrier, inc=1, device_id={"dp": lax.rem(dp + k, n_dp)}, device_id_type=MESH)

    idv = ids[...]
    tall = -(-n_e // 16) * 16
    level = lax.broadcasted_iota(jnp.int32, (tall, rows), 0)
    hots = [(level == idv[k:k + 1, :]).astype(F32) for k in range(top)]
    above = lax.broadcasted_iota(jnp.int32, (rows, rows), 0) < lax.broadcasted_iota(jnp.int32, (rows, rows), 1)
    rank = dot(sum(hots[1:], hots[0]).astype(BF16), above.astype(BF16))
    slot_level = lax.broadcasted_iota(jnp.int32, (slots, rows), 0)
    where = []
    for k in range(top):
        slot = jnp.sum(hots[k] * rank, axis=0, keepdims=True).astype(jnp.int32)
        where.append((slot_level == idv[k:k + 1, :] * cap + slot).astype(F32))
    spread = sum(where[1:], where[0]).astype(BF16)

    pieces = [pl.ds(pl.multiple_of(flip(me, k, n_e) * cap, cap), cap) for k in range(n_e)]
    order = list(range(n_e - 1, 0, -1))

    def exchange(phase, src, dst):
        own = pltpu.make_async_copy(src.at[pieces[0]], dst.at[pieces[0]], own_sem.at[phase])
        copies = [
            pltpu.make_async_remote_copy(
                src_ref=src.at[pieces[k]], dst_ref=dst.at[pieces[0]],
                send_sem=ssem.at[phase, k], recv_sem=rsem.at[phase, k],
                device_id={"expert": flip(me, k, n_e)}, device_id_type=MESH,
            )
            for k in order
        ]
        for copy in copies:
            copy.start()
        own.start()
        return own, copies

    def arrived(pair):
        pair[0].wait()
        for copy in pair[1]:
            copy.wait_recv()

    def block(i):
        return pl.ds(pl.multiple_of(i * rows, rows), rows)

    loads[0].wait()
    loads[1].wait()
    latent = dot(tokens[...], w_in[...]).astype(BF16)
    z_send[...] = dot(spread, latent).astype(BF16)
    pl.semaphore_wait(barrier, n_e + n_dp - 2)
    z_pair = exchange(0, z_send, z_recv)
    loads[2].wait()
    loads[3].wait()
    lat_grad[...] = dot(dy[...], w_out[...], 1, 1).astype(BF16)
    g_send[...] = dot(spread, lat_grad[...]).astype(BF16)
    g_pair = exchange(1, g_send, g_recv)

    slices = []
    for k in range(1, n_dp):
        peer = lax.rem(dp + k, n_dp)
        cols = pl.ds(pl.multiple_of(peer * dw, dw), dw)
        for j, (src, dst) in enumerate(((tokens, tok_all), (dy, dy_all))):
            copy = pltpu.make_async_remote_copy(
                src_ref=src.at[:, cols], dst_ref=dst.at[block(dp)],
                send_sem=tssem.at[j, k], recv_sem=trsem.at[j, k],
                device_id={"dp": peer}, device_id_type=MESH,
            )
            copy.start()
            slices.append(copy)
    mine = pl.ds(pl.multiple_of(dp * dw, dw), dw)
    keep = []
    for j, (src, dst) in enumerate(((tokens, tok_all), (dy, dy_all))):
        copy = pltpu.make_async_copy(src.at[:, mine], dst.at[block(dp)], out_sem.at[j])
        copy.start()
        keep.append(copy)

    for k in range(top):
        q[k] = where[k].T.astype(BF16)
    score = jax.nn.sigmoid(logits[...])
    total = jnp.sum(score, axis=0, keepdims=True)
    gate = score / total
    gate_col = jnp.concatenate([gate, jnp.zeros((128 - top, rows), F32)], axis=0).T

    tile = min(256, hidden)
    loads[4].wait()
    loads[5].wait()
    loads[6].wait()
    arrived(z_pair)
    for t in range(hidden // tile):
        cut = slice(t * tile, (t + 1) * tile)
        a = dot(z_recv[...], wg[:, cut])
        b = dot(z_recv[...], wu[:, cut])
        pre_a[:, cut] = a
        pre_b[:, cut] = b
        hid[:, cut] = (a * jax.nn.sigmoid(a) * b).astype(BF16)
    o_send[...] = dot(hid[...], wd[...]).astype(BF16)
    o_pair = exchange(2, o_send, o_recv)

    arrived(g_pair)
    for t in range(hidden // tile):
        cut = slice(t * tile, (t + 1) * tile)
        h = dot(g_recv[...], wd[cut, :], 1, 1)
        a, b = pre_a[:, cut], pre_b[:, cut]
        sg = jax.nn.sigmoid(a)
        ga[:, cut] = (h * b * sg * (1.0 + a * (1.0 - sg))).astype(BF16)
        gb[:, cut] = (h * a * sg).astype(BF16)
    c_send[...] = (dot(ga[...], wg[...], 1, 1) + dot(gb[...], wu[...], 1, 1)).astype(BF16)
    c_pair = exchange(3, c_send, c_recv)

    def share(own, buf, ss, rs, slot):
        copy = pltpu.make_async_copy(own, buf.at[block(dp)], out_sem.at[slot])
        copy.start()
        keep.append(copy)

        def send(origin, target, k):
            copy = pltpu.make_async_remote_copy(
                src_ref=own if k <= n_x else buf.at[block(origin)], dst_ref=buf.at[block(origin)],
                send_sem=ss.at[k], recv_sem=rs.at[k],
                device_id={"dp": target}, device_id_type=MESH,
            )
            copy.start()
            return copy

        across = [send(dp, lax.rem(x + d, n_x) * 2 + c, d) for d in range(1, n_x)]
        pair = [send(dp, x * 2 + 1 - c, n_x)]
        return across, pair, send

    def pass_on(shared):
        across, pair, send = shared
        for d in range(1, n_x):
            across[d - 1].wait_recv()
            pair.append(send(lax.rem(x - d + n_x, n_x) * 2 + c, x * 2 + 1 - c, n_x + d))
        return across + pair

    arrived(o_pair)
    mixed = jnp.zeros((rows, lat), F32)
    lgf = lat_grad[...].astype(F32)
    lane = lax.broadcasted_iota(jnp.int32, (rows, 128), 1)
    gate_grad = jnp.zeros((rows, 128), F32)
    for k in range(top):
        back = dot(q[k], o_recv[...])
        mixed = mixed + gate_col[:, k:k + 1] * back
        gate_grad = jnp.where(lane == k, jnp.sum(back * lgf, axis=1, keepdims=True), gate_grad)
    mix[...] = mixed.astype(BF16)
    mix_share = share(mix, mix_all, mssem, mrsem, 2)
    gate_grad = gate_grad.T[:top, :]
    mean = jnp.sum(gate * gate_grad, axis=0, keepdims=True)
    logit_grad[...] = score * (1.0 - score) * (gate_grad - mean) / total
    mix_sent = pass_on(mix_share)

    arrived(c_pair)
    total_grad = jnp.zeros((rows, lat), F32)
    for k in range(top):
        total_grad = total_grad + gate_col[:, k:k + 1] * dot(q[k], c_recv[...])
    lg[...] = total_grad.astype(BF16)
    lg_sent = pass_on(share(lg, lg_all, lssem, lrsem, 3))

    for copy in slices + mix_sent[n_x - 1:] + lg_sent[n_x - 1:]:
        copy.wait_recv()
    for pair in (z_pair, g_pair, o_pair, c_pair):
        for copy in pair[1]:
            copy.wait_send()
    for copy in slices + mix_sent + lg_sent:
        copy.wait_send()
    for copy in keep:
        copy.wait()


def last_kernel(
    n_dp, w_in_h, tok_h, dy_h, mix_h, lg_h, part, tg_h, gin_h, gout_h, logit_grad,
    w_in, tok, dy, mix, lg, tg, gin, gout, sem, out_sem,
):
    rows = tg.shape[0]
    loads = []
    for i, (src, dst) in enumerate(((dy_h, dy), (mix_h, mix), (tok_h, tok), (lg_h, lg), (w_in_h, w_in))):
        copy = pltpu.make_async_copy(src, dst, sem.at[i])
        copy.start()
        loads.append(copy)
    logit_grad[...] = part[...]
    dp = lax.axis_index("dp")
    stores = []

    def store(src, dst):
        copy = pltpu.make_async_copy(src, dst, out_sem.at[len(stores)])
        copy.start()
        stores.append(copy)

    loads[0].wait()
    loads[1].wait()
    gout[...] = dot(mix[...], dy[...], 0, 0)
    store(gout, gout_h.at[0])
    loads[2].wait()
    loads[3].wait()
    gin[...] = dot(tok[...], lg[...], 0, 0)
    store(gin, gin_h.at[0])
    loads[4].wait()
    own = lg[pl.ds(pl.multiple_of(dp * rows, rows), rows), :]
    tg[...] = dot(own, w_in[...], 1, 1).astype(BF16)
    store(tg, tg_h)
    for copy in stores:
        copy.wait()


def body(n_e, n_dp, tokens, out_grad, w_in, w_out, w_gate, w_up, w_down, gate_logits, expert_ids):
    rows, width = tokens.shape
    top = expert_ids.shape[1]
    lat = w_in.shape[1]
    hidden = w_gate.shape[2]
    assert w_gate.shape[0] == 1 and n_dp % 2 == 0
    cap = 3 * rows * top // (2 * n_e)
    cap = -(-cap // 16) * 16
    slots = n_e * cap
    dw = width // n_dp
    any_ = pl.BlockSpec(memory_space=pl.ANY)
    vmem = pl.BlockSpec(memory_space=pltpu.VMEM)
    V = pltpu.VMEM
    dma = pltpu.SemaphoreType.DMA
    arrays = pl.pallas_call(
        functools.partial(kernel, n_e, n_dp, cap),
        out_shape=(
            jax.ShapeDtypeStruct((top, rows), F32),
            jax.ShapeDtypeStruct((n_dp * rows, dw), BF16),
            jax.ShapeDtypeStruct((n_dp * rows, dw), BF16),
            jax.ShapeDtypeStruct((n_dp * rows, lat), BF16),
            jax.ShapeDtypeStruct((n_dp * rows, lat), BF16),
        ),
        in_specs=[any_] * 7 + [vmem] * 2,
        out_specs=(vmem, any_, any_, any_, any_),
        scratch_shapes=[
            V((rows, width), BF16), V((rows, width), BF16),
            V((width, lat), BF16), V((lat, width), BF16),
            V((lat, hidden), BF16), V((lat, hidden), BF16), V((hidden, lat), BF16),
            V((top, rows, slots), BF16), V((rows, lat), BF16),
            *[V((slots, lat), BF16)] * 8,
            V((slots, hidden), F32), V((slots, hidden), F32),
            V((slots, hidden), BF16), V((slots, hidden), BF16), V((slots, hidden), BF16),
            V((rows, lat), BF16), V((rows, lat), BF16),
            dma((7,)), dma((4,)), dma((4, n_e)), dma((4, n_e)),
            dma((2, n_dp)), dma((2, n_dp)),
            dma((n_dp,)), dma((n_dp,)), dma((n_dp,)), dma((n_dp,)), dma((4,)),
        ],
        compiler_params=pltpu.CompilerParams(
            collective_id=0, has_side_effects=True, vmem_limit_bytes=48 * 1024 * 1024
        ),
    )(tokens, out_grad, w_in, w_out, w_gate, w_up, w_down, gate_logits.T, expert_ids.T)
    token_grad, grad_in, grad_out, logit_grad = pl.pallas_call(
        functools.partial(last_kernel, n_dp),
        out_shape=(
            jax.ShapeDtypeStruct((rows, width), BF16),
            jax.ShapeDtypeStruct((1, dw, lat), F32),
            jax.ShapeDtypeStruct((1, lat, dw), F32),
            jax.ShapeDtypeStruct((top, rows), F32),
        ),
        in_specs=[any_] * 5 + [vmem],
        out_specs=(any_, any_, any_, vmem),
        scratch_shapes=[
            V((width, lat), BF16),
            V((n_dp * rows, dw), BF16), V((n_dp * rows, dw), BF16),
            V((n_dp * rows, lat), BF16), V((n_dp * rows, lat), BF16),
            V((rows, width), BF16), V((dw, lat), F32), V((lat, dw), F32),
            dma((5,)), dma((3,)),
        ],
        compiler_params=pltpu.CompilerParams(vmem_limit_bytes=24 * 1024 * 1024),
    )(w_in, *arrays[1:], arrays[0])
    return token_grad, logit_grad.T, grad_in, grad_out


def solution(mesh):
    placed = (
        P(("dp", "expert"), None),
        P(("dp", "expert"), None),
        P(),
        P(),
        P("expert", None, None),
        P("expert", None, None),
        P("expert", None, None),
        P(("dp", "expert"), None),
        P(("dp", "expert"), None),
    )
    return jax.shard_map(
        functools.partial(body, mesh.shape["expert"], mesh.shape["dp"]),
        mesh=mesh,
        in_specs=placed,
        out_specs=(
            P(("dp", "expert"), None),
            P(("dp", "expert"), None),
            P("expert", "dp", None),
            P("expert", None, "dp"),
        ),
        check_vma=False,
    )
```

```python
import functools

import jax
import jax.numpy as jnp
from jax import lax
from jax.experimental import pallas as pl
from jax.experimental.pallas import tpu as pltpu
from jax.sharding import PartitionSpec as P

BF16 = jnp.bfloat16
F32 = jnp.float32
MESH = pl.DeviceIdType.MESH


def dot(a, b, ca=1, cb=0):
    return lax.dot_general(a, b, (((ca,), (cb,)), ((), ())), preferred_element_type=F32)


def flip(me, k, n):
    out, bit = 0, 1
    while bit < n:
        mine = lax.rem(me // bit, 2)
        out = out + (1 - mine if (k // bit) % 2 else mine) * bit
        bit *= 2
    return out


def kernel(
    n_e, n_dp, cap,
    tokens_h, dy_h, w_in_h, w_out_h, wg_h, wu_h, wd_h, logits_h, ids_h,
    logit_grad, tok_all, dy_all, mix_all, lg_all,
    tokens, dy, w_in, w_out, wg, wu, wd,
    q, lat_grad,
    z_send, g_send, o_send, c_send, z_recv, g_recv, o_recv, c_recv,
    pre_a, pre_b, hid, ga, gb,
    mix, lg, logits, ids,
    load_sem, own_sem, ssem, rsem, tssem, trsem, mssem, mrsem, lssem, lrsem, out_sem,
):
    top, rows = ids.shape
    slots = n_e * cap
    lat = w_in.shape[1]
    hidden = wg.shape[1]
    dw = tok_all.shape[1]
    me = lax.axis_index("expert")
    dp = lax.axis_index("dp")
    n_x = n_dp // 2
    x, c = dp // 2, lax.rem(dp, 2)

    loads = []
    for i, (src, dst) in enumerate((
        (ids_h, ids), (logits_h, logits), (tokens_h, tokens), (w_in_h, w_in), (dy_h, dy), (w_out_h, w_out),
        (wg_h.at[0], wg), (wu_h.at[0], wu), (wd_h.at[0], wd),
    )):
        load = pltpu.make_async_copy(src, dst, load_sem.at[i])
        if i < 4:
            load.start()
        loads.append(load)

    barrier = pltpu.get_barrier_semaphore()
    for k in range(1, n_e):
        pl.semaphore_signal(barrier, inc=1, device_id={"expert": flip(me, k, n_e)}, device_id_type=MESH)
    for k in range(1, n_dp):
        pl.semaphore_signal(barrier, inc=1, device_id={"dp": lax.rem(dp + k, n_dp)}, device_id_type=MESH)

    loads[0].wait()
    idv = ids[...]
    tall = -(-n_e // 16) * 16
    level = lax.broadcasted_iota(jnp.int32, (tall, rows), 0)
    hots = [(level == idv[k:k + 1, :]).astype(F32) for k in range(top)]
    above = lax.broadcasted_iota(jnp.int32, (rows, rows), 0) < lax.broadcasted_iota(jnp.int32, (rows, rows), 1)
    rank = dot(sum(hots[1:], hots[0]).astype(BF16), above.astype(BF16))
    slot_level = lax.broadcasted_iota(jnp.int32, (slots, rows), 0)
    where = []
    for k in range(top):
        slot = jnp.sum(hots[k] * rank, axis=0, keepdims=True).astype(jnp.int32)
        where.append((slot_level == idv[k:k + 1, :] * cap + slot).astype(F32))
    spread = sum(where[1:], where[0]).astype(BF16)

    pieces = [pl.ds(pl.multiple_of(flip(me, k, n_e) * cap, cap), cap) for k in range(n_e)]
    order = list(range(n_e - 1, 0, -1))

    def exchange(phase, src, dst):
        own = pltpu.make_async_copy(src.at[pieces[0]], dst.at[pieces[0]], own_sem.at[phase])
        copies = [
            pltpu.make_async_remote_copy(
                src_ref=src.at[pieces[k]], dst_ref=dst.at[pieces[0]],
                send_sem=ssem.at[phase, k], recv_sem=rsem.at[phase, k],
                device_id={"expert": flip(me, k, n_e)}, device_id_type=MESH,
            )
            for k in order
        ]
        for copy in copies:
            copy.start()
        own.start()
        return own, copies

    def arrived(pair):
        pair[0].wait()
        for copy in pair[1]:
            copy.wait_recv()

    def block(i):
        return pl.ds(pl.multiple_of(i * rows, rows), rows)

    loads[2].wait()
    loads[3].wait()
    for load in loads[4:]:
        load.start()
    latent = dot(tokens[...], w_in[...]).astype(BF16)
    z_send[...] = dot(spread, latent).astype(BF16)
    pl.semaphore_wait(barrier, n_e + n_dp - 2)
    z_pair = exchange(0, z_send, z_recv)
    loads[4].wait()
    loads[5].wait()
    lat_grad[...] = dot(dy[...], w_out[...], 1, 1).astype(BF16)
    g_send[...] = dot(spread, lat_grad[...]).astype(BF16)
    g_pair = exchange(1, g_send, g_recv)

    slices = []
    for k in range(1, n_dp):
        peer = lax.rem(dp + k, n_dp)
        cols = pl.ds(pl.multiple_of(peer * dw, dw), dw)
        for j, (src, dst) in enumerate(((tokens, tok_all), (dy, dy_all))):
            copy = pltpu.make_async_remote_copy(
                src_ref=src.at[:, cols], dst_ref=dst.at[block(dp)],
                send_sem=tssem.at[j, k], recv_sem=trsem.at[j, k],
                device_id={"dp": peer}, device_id_type=MESH,
            )
            copy.start()
            slices.append(copy)
    mine = pl.ds(pl.multiple_of(dp * dw, dw), dw)
    keep = []
    for j, (src, dst) in enumerate(((tokens, tok_all), (dy, dy_all))):
        copy = pltpu.make_async_copy(src.at[:, mine], dst.at[block(dp)], out_sem.at[j])
        copy.start()
        keep.append(copy)

    for k in range(top):
        q[k] = where[k].T.astype(BF16)
    loads[1].wait()
    score = jax.nn.sigmoid(logits[...])
    total = jnp.sum(score, axis=0, keepdims=True)
    gate = score / total
    gate_col = jnp.concatenate([gate, jnp.zeros((128 - top, rows), F32)], axis=0).T

    tile = min(256, hidden)
    loads[6].wait()
    loads[7].wait()
    loads[8].wait()
    arrived(z_pair)
    for t in range(hidden // tile):
        cut = slice(t * tile, (t + 1) * tile)
        a = dot(z_recv[...], wg[:, cut])
        b = dot(z_recv[...], wu[:, cut])
        pre_a[:, cut] = a
        pre_b[:, cut] = b
        hid[:, cut] = (a * jax.nn.sigmoid(a) * b).astype(BF16)
    o_send[...] = dot(hid[...], wd[...]).astype(BF16)
    o_pair = exchange(2, o_send, o_recv)

    arrived(g_pair)
    for t in range(hidden // tile):
        cut = slice(t * tile, (t + 1) * tile)
        h = dot(g_recv[...], wd[cut, :], 1, 1)
        a, b = pre_a[:, cut], pre_b[:, cut]
        sg = jax.nn.sigmoid(a)
        ga[:, cut] = (h * b * sg * (1.0 + a * (1.0 - sg))).astype(BF16)
        gb[:, cut] = (h * a * sg).astype(BF16)
    c_send[...] = (dot(ga[...], wg[...], 1, 1) + dot(gb[...], wu[...], 1, 1)).astype(BF16)
    c_pair = exchange(3, c_send, c_recv)

    def share(own, buf, ss, rs, slot):
        copy = pltpu.make_async_copy(own, buf.at[block(dp)], out_sem.at[slot])
        copy.start()
        keep.append(copy)

        def send(origin, target, k):
            copy = pltpu.make_async_remote_copy(
                src_ref=own if k <= n_x else buf.at[block(origin)], dst_ref=buf.at[block(origin)],
                send_sem=ss.at[k], recv_sem=rs.at[k],
                device_id={"dp": target}, device_id_type=MESH,
            )
            copy.start()
            return copy

        across = [send(dp, lax.rem(x + d, n_x) * 2 + c, d) for d in range(1, n_x)]
        pair = [send(dp, x * 2 + 1 - c, n_x)]
        return across, pair, send

    def pass_on(shared):
        across, pair, send = shared
        for d in range(1, n_x):
            across[d - 1].wait_recv()
            pair.append(send(lax.rem(x - d + n_x, n_x) * 2 + c, x * 2 + 1 - c, n_x + d))
        return across + pair

    arrived(o_pair)
    mixed = jnp.zeros((rows, lat), F32)
    lgf = lat_grad[...].astype(F32)
    lane = lax.broadcasted_iota(jnp.int32, (rows, 128), 1)
    gate_grad = jnp.zeros((rows, 128), F32)
    for k in range(top):
        back = dot(q[k], o_recv[...])
        mixed = mixed + gate_col[:, k:k + 1] * back
        gate_grad = jnp.where(lane == k, jnp.sum(back * lgf, axis=1, keepdims=True), gate_grad)
    mix[...] = mixed.astype(BF16)
    mix_share = share(mix, mix_all, mssem, mrsem, 2)
    gate_grad = gate_grad.T[:top, :]
    mean = jnp.sum(gate * gate_grad, axis=0, keepdims=True)
    logit_grad[...] = score * (1.0 - score) * (gate_grad - mean) / total
    mix_sent = pass_on(mix_share)

    arrived(c_pair)
    total_grad = jnp.zeros((rows, lat), F32)
    for k in range(top):
        total_grad = total_grad + gate_col[:, k:k + 1] * dot(q[k], c_recv[...])
    lg[...] = total_grad.astype(BF16)
    lg_sent = pass_on(share(lg, lg_all, lssem, lrsem, 3))

    for copy in slices + mix_sent[n_x - 1:] + lg_sent[n_x - 1:]:
        copy.wait_recv()
    for pair in (z_pair, g_pair, o_pair, c_pair):
        for copy in pair[1]:
            copy.wait_send()
    for copy in slices + mix_sent + lg_sent:
        copy.wait_send()
    for copy in keep:
        copy.wait()


def last_kernel(
    n_dp, w_in_h, tok_h, dy_h, mix_h, lg_h, part, tg_h, gin_h, gout_h, logit_grad,
    w_in, tok, dy, mix, lg, tg, gin, gout, sem, out_sem,
):
    rows = tg.shape[0]
    loads = []
    for i, (src, dst) in enumerate(((dy_h, dy), (mix_h, mix), (tok_h, tok), (lg_h, lg), (w_in_h, w_in))):
        copy = pltpu.make_async_copy(src, dst, sem.at[i])
        copy.start()
        loads.append(copy)
    logit_grad[...] = part[...]
    dp = lax.axis_index("dp")
    stores = []

    def store(src, dst):
        copy = pltpu.make_async_copy(src, dst, out_sem.at[len(stores)])
        copy.start()
        stores.append(copy)

    loads[0].wait()
    loads[1].wait()
    gout[...] = dot(mix[...], dy[...], 0, 0)
    store(gout, gout_h.at[0])
    loads[2].wait()
    loads[3].wait()
    gin[...] = dot(tok[...], lg[...], 0, 0)
    store(gin, gin_h.at[0])
    loads[4].wait()
    own = lg[pl.ds(pl.multiple_of(dp * rows, rows), rows), :]
    tg[...] = dot(own, w_in[...], 1, 1).astype(BF16)
    store(tg, tg_h)
    for copy in stores:
        copy.wait()


def body(n_e, n_dp, tokens, out_grad, w_in, w_out, w_gate, w_up, w_down, gate_logits, expert_ids):
    rows, width = tokens.shape
    top = expert_ids.shape[1]
    lat = w_in.shape[1]
    hidden = w_gate.shape[2]
    assert w_gate.shape[0] == 1 and n_dp % 2 == 0
    cap = 3 * rows * top // (2 * n_e)
    cap = -(-cap // 16) * 16
    slots = n_e * cap
    dw = width // n_dp
    any_ = pl.BlockSpec(memory_space=pl.ANY)
    hbm = pl.BlockSpec(memory_space=pltpu.HBM)
    vmem = pl.BlockSpec(memory_space=pltpu.VMEM)
    V = pltpu.VMEM
    dma = pltpu.SemaphoreType.DMA
    arrays = pl.pallas_call(
        functools.partial(kernel, n_e, n_dp, cap),
        out_shape=(
            jax.ShapeDtypeStruct((top, rows), F32),
            jax.ShapeDtypeStruct((n_dp * rows, dw), BF16),
            jax.ShapeDtypeStruct((n_dp * rows, dw), BF16),
            jax.ShapeDtypeStruct((n_dp * rows, lat), BF16),
            jax.ShapeDtypeStruct((n_dp * rows, lat), BF16),
        ),
        in_specs=[hbm] * 9,
        out_specs=(vmem, any_, any_, any_, any_),
        scratch_shapes=[
            V((rows, width), BF16), V((rows, width), BF16),
            V((width, lat), BF16), V((lat, width), BF16),
            V((lat, hidden), BF16), V((lat, hidden), BF16), V((hidden, lat), BF16),
            V((top, rows, slots), BF16), V((rows, lat), BF16),
            *[V((slots, lat), BF16)] * 8,
            V((slots, hidden), F32), V((slots, hidden), F32),
            V((slots, hidden), BF16), V((slots, hidden), BF16), V((slots, hidden), BF16),
            V((rows, lat), BF16), V((rows, lat), BF16), V((top, rows), F32), V((top, rows), jnp.int32),
            dma((9,)), dma((4,)), dma((4, n_e)), dma((4, n_e)),
            dma((2, n_dp)), dma((2, n_dp)),
            dma((n_dp,)), dma((n_dp,)), dma((n_dp,)), dma((n_dp,)), dma((4,)),
        ],
        compiler_params=pltpu.CompilerParams(
            collective_id=0, has_side_effects=True, vmem_limit_bytes=56 * 1024 * 1024
        ),
    )(tokens, out_grad, w_in, w_out, w_gate, w_up, w_down, gate_logits.T, expert_ids.T)
    token_grad, grad_in, grad_out, logit_grad = pl.pallas_call(
        functools.partial(last_kernel, n_dp),
        out_shape=(
            jax.ShapeDtypeStruct((rows, width), BF16),
            jax.ShapeDtypeStruct((1, dw, lat), F32),
            jax.ShapeDtypeStruct((1, lat, dw), F32),
            jax.ShapeDtypeStruct((top, rows), F32),
        ),
        in_specs=[any_] * 5 + [vmem],
        out_specs=(any_, any_, any_, vmem),
        scratch_shapes=[
            V((width, lat), BF16),
            V((n_dp * rows, dw), BF16), V((n_dp * rows, dw), BF16),
            V((n_dp * rows, lat), BF16), V((n_dp * rows, lat), BF16),
            V((rows, width), BF16), V((dw, lat), F32), V((lat, dw), F32),
            dma((5,)), dma((3,)),
        ],
        compiler_params=pltpu.CompilerParams(vmem_limit_bytes=58 * 1024 * 1024),
    )(w_in, *arrays[1:], arrays[0])
    return token_grad, logit_grad.T, grad_in, grad_out


def solution(mesh):
    placed = (
        P(("dp", "expert"), None),
        P(("dp", "expert"), None),
        P(),
        P(),
        P("expert", None, None),
        P("expert", None, None),
        P("expert", None, None),
        P(("dp", "expert"), None),
        P(("dp", "expert"), None),
    )
    return jax.shard_map(
        functools.partial(body, mesh.shape["expert"], mesh.shape["dp"]),
        mesh=mesh,
        in_specs=placed,
        out_specs=(
            P(("dp", "expert"), None),
            P(("dp", "expert"), None),
            P("expert", "dp", None),
            P("expert", None, "dp"),
        ),
        check_vma=False,
    )
```
